32 devices in a mesh: facet: 8 (over z, x), col: 4 (over y, core).
Axes of the slice: x: 2, y: 2, z: 4, core: 2. Of those that a mesh axis runs over, the one named last changes fastest.
Arguments:
- strips: bfloat16 [32768, 512], P('facet', 'col'), may hold values from -6 to 6
- offsets: int32 [4, 8], P('col'), may hold values from 0 to 4095
- vis_subgrid: int32 [16384], P(('facet', 'col')), may hold values from 0 to 31, as said below
- vis_uv: int32 [16384], P(('facet', 'col')), may hold values from 0 to 262143
- observed: float32 [16384], P(('facet', 'col')), may hold values from -6 to 6
- weights: float32 [16384], P(('facet', 'col')), may hold values from 0.25 to 1
Outputs:
- facet_residual: float32 [32768, 512], P('facet', 'col')
The draws below stay inside these ranges and needn't reach their ends.
Inputs may be any that keep to these rules, and one draw needn't show every extreme that they name: `vis_subgrid`: within each device's aligned block of 512 visibilities no subgrid is named more than 32 times, and one subgrid, the same for all blocks, is named exactly 32 times in every block.
All inputs are finite; a program needn't handle non-finite values.
Results may differ from the reference program's by a relative error of at most 0.01.
Values may be sent and summed in bfloat16 or wider, within the bound.
A program may use at most 128 MiB of HBM per device.

```python
import math
import jax
import jax.numpy as jnp
from jax import lax

K = 128
SG = 512
FR = 4096
VIS_DEV = 512
NSC = 8
COLUMNS = 4
SUBGRIDS = 32
CAPV = 32
VIS_SUB = 1024
TOTAL_VIS = 16384
N_FACET = 8


def draw_vis_subgrid(key, part):
    hot_key, block_key = jax.random.split(jax.random.fold_in(key, 7))
    hot_id = jax.random.randint(hot_key, (), 0, SUBGRIDS).astype(jnp.int32)
    slot_ids = jnp.arange((SUBGRIDS - 1) * CAPV, dtype=jnp.int32) // CAPV
    others = slot_ids + (slot_ids >= hot_id).astype(jnp.int32)

    def one_block(block_seed):
        pick_key, second = jax.random.split(block_seed)
        chosen = jax.random.permutation(pick_key, others)[:VIS_DEV - CAPV]
        block_ids = jnp.concatenate([jnp.full((CAPV,), hot_id, jnp.int32), chosen])
        return jax.random.permutation(second, block_ids)
    block_keys = jax.random.split(block_key, TOTAL_VIS // VIS_DEV)
    return jax.vmap(one_block)(block_keys).reshape(-1).astype(jnp.int32)


def with_ends(array, rng, smallest, largest):
    place = [jax.random.randint(jax.random.fold_in(rng, axis), (), 0, length) for axis, length in enumerate(array.shape)]
    widest = array.shape.index(max(array.shape))
    beside = place[:widest] + [(place[widest] + 1) % array.shape[widest]] + place[widest + 1:]
    return array.at[tuple(place)].set(smallest).at[tuple(beside)].set(largest)


def level_of(own_key, dims, cuts, least, top_value):
    def one(axis_at, shards_of):
        heights = jax.random.uniform(jax.random.fold_in(jax.random.fold_in(own_key, 6), axis_at), (shards_of,), jnp.float32, least / len(cuts), top_value / len(cuts))
        return jnp.repeat(jnp.exp(heights), dims[axis_at] // shards_of).reshape((-1,) + (1,) * (len(dims) - axis_at - 1))

    gain = one(*cuts[0])
    for cut in cuts[1:]:
        gain = gain * one(*cut)
    return gain


def noise(rng, shape, scale, bound, cuts=(), held_as=jnp.bfloat16):
    array = scale * jax.random.normal(rng, shape, jnp.float32)
    if cuts:
        array = array * level_of(rng, shape, cuts, -0.22, 0.18)
    return jnp.clip(array, -bound, bound).astype(held_as)


def setup_inputs(seed: int = 0) -> dict:
    seeds = jax.random.split(jax.random.key(seed), 7)
    return {
        "strips": noise(seeds[0], (N_FACET * FR, COLUMNS * K), 1.0, 6.0, ((0, 8), (1, 4))),
        "offsets": with_ends(jax.random.randint(seeds[1], (COLUMNS, NSC), 0, FR), jax.random.fold_in(seeds[1], 1), 0, FR - 1).astype(jnp.int32),
        "vis_subgrid": draw_vis_subgrid(jax.random.fold_in(seeds[6], 71), 0),
        "vis_uv": with_ends(jax.random.randint(seeds[3], (TOTAL_VIS,), 0, SG * SG), jax.random.fold_in(seeds[3], 1), 0, (SG * SG) - 1).astype(jnp.int32),
        "observed": noise(seeds[4], (TOTAL_VIS,), 1.0, 6.0, ((0, 32),), jnp.float32),
        "weights": jnp.clip(jnp.exp(math.log(1.0) - 1.3862944 * jax.random.uniform(seeds[5], (TOTAL_VIS,), jnp.float32) ** level_of(seeds[5], (TOTAL_VIS,), ((0, 32),), -0.2, 0.2)), 0.25, 1.0),
    }


two_pi = 2.0 * math.pi

def facet_table(offset_value, rows_total, width):
    row_index = lax.iota(jnp.int32, rows_total)
    freq_index = lax.iota(jnp.int32, width)
    phase_int = (offset_value + freq_index[:, None]) * row_index[None, :] % rows_total
    angle = two_pi * phase_int.astype(jnp.float32) / rows_total
    taper = 0.6 - 0.4 * jnp.cos(two_pi * row_index.astype(jnp.float32) / rows_total)
    return (taper[None, :] * (jnp.cos(angle) + jnp.sin(angle)) / math.sqrt(rows_total)).astype(jnp.bfloat16)

def kernel_rows(coord, sub_size):
    pixel = lax.iota(jnp.int32, sub_size)
    phase_int = coord[:, None] * pixel[None, :] % sub_size
    angle = two_pi * phase_int.astype(jnp.float32) / sub_size
    return ((jnp.cos(angle) + jnp.sin(angle)) / math.sqrt(sub_size)).astype(jnp.bfloat16)

def reference(strips, offsets, vis_subgrid, vis_uv, observed, weights):
    order = jnp.argsort(vis_subgrid, stable=True).astype(jnp.int32)
    counts = jnp.bincount(vis_subgrid, length=SUBGRIDS).astype(jnp.int32)
    starts = (jnp.cumsum(counts) - counts).astype(jnp.int32)
    quarter = NSC // 4
    outputs = []
    for column in range(COLUMNS):
        strip_cols = strips[:, column * K:(column + 1) * K].reshape(NSC, FR, K)
        strip_cols = jnp.transpose(strip_cols, (1, 0, 2)).reshape(FR, NSC * K)

        def per_owner(total, inputs):
            offset_value, owner = inputs
            table = facet_table(offset_value, FR, K)
            contrib = jnp.dot(table, strip_cols, preferred_element_type=jnp.float32).astype(jnp.bfloat16)
            subgrid = jnp.zeros((SG, SG), jnp.float32)
            for facet in range(NSC):
                row_start = facet % 4 * (SG // 4)
                col_start = facet // 4 * SG // quarter
                target = ((col_start + jnp.arange(K)) % SG).astype(jnp.int32)
                block_f = contrib[:, facet * K:(facet + 1) * K].astype(jnp.float32)
                subgrid = subgrid.at[row_start:row_start + K, target].add(block_f)
            subgrid = subgrid.astype(jnp.bfloat16)
            number = owner * COLUMNS + column
            position = lax.iota(jnp.int32, VIS_SUB)
            valid = position < counts[number]
            picked = order[jnp.minimum(starts[number] + position, TOTAL_VIS - 1)]
            uv_sel = jnp.where(valid, vis_uv[picked], 0).astype(jnp.int32)
            obs_sel = jnp.where(valid, observed[picked], jnp.float32(0.0))
            weight_sel = jnp.where(valid, weights[picked], jnp.float32(0.0))
            row_kernel = kernel_rows(uv_sel // SG, SG)
            col_kernel = kernel_rows(uv_sel % SG, SG)
            product_rows = jnp.dot(row_kernel, subgrid, preferred_element_type=jnp.float32)
            predicted = lax.optimization_barrier(jnp.sum(product_rows * col_kernel.astype(jnp.float32), axis=1))
            weighted = weight_sel * (obs_sel - predicted)
            spread = (weighted[:, None] * col_kernel.astype(jnp.float32)).astype(jnp.bfloat16)
            residual_grid = (math.sqrt(SG) * jnp.dot(row_kernel.T, spread, preferred_element_type=jnp.float32)).astype(jnp.bfloat16)
            pieces = []
            for facet in range(NSC):
                row_start = facet % 4 * (SG // 4)
                col_start = facet // 4 * SG // quarter
                target = ((col_start + jnp.arange(K)) % SG).astype(jnp.int32)
                pieces.append(residual_grid[row_start:row_start + K][:, target])
            returned = jnp.concatenate(pieces, axis=1)
            total = total + jnp.dot(table.T, returned, preferred_element_type=jnp.float32)
            return (total, None)
        start_total = jnp.zeros((FR, NSC * K), jnp.float32)
        owners = lax.iota(jnp.int32, NSC)
        total, unused = lax.scan(per_owner, start_total, (offsets[column], owners))
        total = jnp.transpose(total.reshape(FR, NSC, K), (1, 0, 2)).reshape(NSC * FR, K)
        outputs.append(total)
    return jnp.concatenate(outputs, axis=1)
```

```python
import functools
import math

import jax
import jax.numpy as jnp
import numpy as np
from jax import lax
from jax.experimental import pallas as pl
from jax.experimental.pallas import tpu as pltpu
from jax.sharding import PartitionSpec as P

SG = 512
LANES = 128
VALS = 8


def cas_tables(rows_total, width):
    phase = np.arange(width)[:, None] * np.arange(rows_total)[None, :] % rows_total
    angle = 2.0 * np.pi * phase / rows_total
    taper = (0.6 - 0.4 * np.cos(2.0 * np.pi * np.arange(rows_total) / rows_total)) / math.sqrt(
        rows_total
    )
    cas = (np.cos(angle) + np.sin(angle)).astype(np.float32)
    dif = (np.cos(angle) - np.sin(angle)).astype(np.float32)
    return cas, dif, taper.astype(np.float32)[None, :]


def grid_tables(quarter, width, sub_size):
    phase = np.arange(sub_size)[:, None] * np.arange(sub_size)[None, :] % sub_size
    angle = 2.0 * np.pi * phase / sub_size
    cas = ((np.cos(angle) + np.sin(angle)) / math.sqrt(sub_size)).astype(jnp.bfloat16)
    start = np.arange(quarter) * sub_size // quarter
    target = (start[:, None] + np.arange(width)[None, :]).reshape(-1) % sub_size
    return cas, cas[target]


def sin_cos(turn):
    quad = jnp.floor(4.0 * turn + 0.5)
    x = (turn - 0.25 * quad) * (2.0 * math.pi)
    y = x * x
    s = x * (1.0 + y * (-1.0 / 6 + y * (1.0 / 120 + y * (-1.0 / 5040 + y * (1.0 / 362880)))))
    c = 1.0 + y * (-0.5 + y * (1.0 / 24 + y * (-1.0 / 720 + y * (1.0 / 40320))))
    one, two, three = quad == 1.0, quad == 2.0, quad == 3.0
    sine = jnp.where(one, c, jnp.where(two, -s, jnp.where(three, -c, s)))
    cosine = jnp.where(one, -s, jnp.where(two, -c, jnp.where(three, s, c)))
    return sine, cosine


def kernel(
    n, ncol, cap,
    strips, offs, vsub, vuv, obs, wts, cas, dif, taper, ctab, cplace,
    out,
    atab, cos_rows, sin_rows, vsend, vrecv, csend, crecv, rsend, rrecv,
    vis, hot_u, hot_v, hot_w, grid_s, grid_f, ret_t,
    vs_sem, vr_sem, cs_sem, cr_sem, rs_sem, rr_sem,
):
    rows_total, width = strips.shape
    devices = n * ncol
    quarter = n // 4
    nvis = vsub.shape[1]
    group = LANES // cap
    groups = devices // group
    me = lax.axis_index("facet")
    my_col = lax.axis_index("col")
    flat = me * ncol + my_col
    f32, bf16 = jnp.float32, jnp.bfloat16

    barrier = pltpu.get_barrier_semaphore()

    def greet(d, carry):
        t = lax.rem(flat + d, devices)
        pl.semaphore_signal(
            barrier, inc=1, device_id={"facet": t // ncol, "col": lax.rem(t, ncol)},
            device_id_type=pl.DeviceIdType.MESH,
        )
        return carry

    lax.fori_loop(1, devices, greet, 0)

    sub = vsub[...]
    hits = lax.broadcasted_iota(jnp.int32, (devices, nvis), 0) == sub
    hits_f = jnp.where(hits, 1.0, 0.0).astype(f32)
    before = (
        lax.broadcasted_iota(jnp.int32, (nvis, nvis), 0)
        < lax.broadcasted_iota(jnp.int32, (nvis, nvis), 1)
    )
    before = jnp.where(before, 1.0, 0.0).astype(bf16)
    counts = jnp.dot(hits_f.astype(bf16), before, preferred_element_type=f32)
    rank = jnp.sum(counts * hits_f, axis=0, keepdims=True)
    lane = rank + (lax.rem(flat, group) * cap).astype(f32)
    slots = lax.broadcasted_iota(jnp.int32, (LANES, nvis), 0).astype(f32) == lane
    slots = jnp.where(slots, 1.0, 0.0).astype(f32)
    uv = vuv[...]
    pu = (uv // SG).astype(f32)
    pv = (uv % SG).astype(f32)
    vals = jnp.concatenate(
        [pu, pv, obs[...], wts[...], jnp.zeros((VALS - 4, nvis), f32)], axis=0
    )
    left = hits_f[:, None, :] * vals[None, :, :]
    packed = lax.dot_general(
        left.reshape(devices * VALS, nvis), slots, (((1,), (1,)), ((), ())),
        precision=lax.Precision.HIGHEST, preferred_element_type=f32,
    )
    vsend[...] = packed.reshape(devices, VALS, LANES)
    vrecv[flat] = vsend[flat]

    row = lax.broadcasted_iota(jnp.int32, (n, rows_total), 1)
    turn = ((offs[...] * row) % rows_total).astype(f32) * (1.0 / rows_total)
    sine, cosine = sin_cos(turn)
    cos_rows[...] = (cosine * taper[...]).reshape(n, 1, rows_total)
    sin_rows[...] = (sine * taper[...]).reshape(n, 1, rows_total)

    pl.semaphore_wait(barrier, devices - 1)

    def vis_copy(to, source):
        return pltpu.make_async_remote_copy(
            src_ref=vsend.at[to], dst_ref=vrecv.at[source],
            send_sem=vs_sem.at[to], recv_sem=vr_sem.at[source],
            device_id={"facet": to // ncol, "col": lax.rem(to, ncol)},
            device_id_type=pl.DeviceIdType.MESH,
        )

    def block_copy(send, recv, s_sem, r_sem, to, source):
        return pltpu.make_async_remote_copy(
            src_ref=send.at[to], dst_ref=recv.at[source],
            send_sem=s_sem.at[to], recv_sem=r_sem.at[source],
            device_id={"facet": to}, device_id_type=pl.DeviceIdType.MESH,
        )

    def send_vis(d, carry):
        vis_copy(lax.rem(flat + d, devices), flat).start()
        return carry

    lax.fori_loop(1, devices, send_vis, 0)

    chunk = min(512, rows_total)

    def one_owner(i, carry):
        o = lax.rem(me + 1 + i, n)
        at = pl.ds(pl.multiple_of(o * width, width), width)
        acc = jnp.zeros((width, strips.shape[1]), f32)
        for c in range(rows_total // chunk):
            cols = pl.ds(c * chunk, chunk)
            mixed = cos_rows[o, :, cols] * cas[:, cols] + sin_rows[o, :, cols] * dif[:, cols]
            mixed = mixed.astype(bf16)
            atab[at, cols] = mixed
            acc = acc + jnp.dot(mixed, strips[cols, :], preferred_element_type=f32)
        csend[o] = acc.astype(bf16)

        @pl.when(i < n - 1)
        def _():
            block_copy(csend, crecv, cs_sem, cr_sem, o, me).start()

        return carry

    lax.fori_loop(0, n, one_owner, 0)
    crecv[me] = csend[me]

    def wait_vis(d, carry):
        vis_copy(flat, lax.rem(flat + d, devices)).wait_recv()
        return carry

    lax.fori_loop(1, devices, wait_vis, 0)
    for g in range(groups):
        vis[:, g * LANES:(g + 1) * LANES] = jnp.sum(vrecv[g * group:(g + 1) * group], axis=0)
    total = groups * LANES
    step = min(256, total)
    pixel = lax.broadcasted_iota(jnp.int32, (SG, step), 0).astype(f32)
    for v in range(total // step):
        span = slice(v * step, (v + 1) * step)
        hot_u[:, span] = jnp.where(pixel == vis[0:1, span], 1.0, 0.0).astype(bf16)
        hot_v[:, span] = jnp.where(pixel == vis[1:2, span], 1.0, 0.0).astype(bf16)

    def wait_block(send, recv, s_sem, r_sem):
        def body(d, carry):
            block_copy(send, recv, s_sem, r_sem, me, lax.rem(me + n - d, n)).wait_recv()
            return carry

        lax.fori_loop(1, n, body, 0)

    wait_block(csend, crecv, cs_sem, cr_sem)
    for f in range(n):
        q, b = f // 4, f % 4
        grid_s[b * width:(b + 1) * width, q * width:(q + 1) * width] = crecv[f]
    half = jnp.dot(ctab[...], grid_s[...], preferred_element_type=f32).astype(bf16)
    grid_f[...] = jnp.dot(half, cplace[...], preferred_element_type=f32).astype(bf16)

    def residual(v, carry):
        span = pl.ds(pl.multiple_of(v * step, step), step)
        rows = jnp.dot(grid_f[...], hot_v[:, span], preferred_element_type=f32)
        predicted = jnp.sum(rows * hot_u[:, span].astype(f32), axis=0, keepdims=True)
        weighted = vis[3:4, span] * (vis[2:3, span] - predicted)
        hot_w[:, span] = (hot_v[:, span].astype(f32) * weighted).astype(bf16)
        return carry

    lax.fori_loop(0, total // step, residual, 0)
    weight_t = lax.dot_general(
        hot_w[...], hot_u[...], (((1,), (1,)), ((), ())), preferred_element_type=f32
    ).astype(bf16)
    grid_g = jnp.dot(weight_t, ctab[...], preferred_element_type=f32).astype(bf16)
    for q in range(quarter):
        part = jnp.dot(
            cplace[q * width:(q + 1) * width, :], grid_g, preferred_element_type=f32
        )
        part = (part * math.sqrt(SG)).astype(bf16)
        for b in range(4):
            f = q * 4 + b
            rsend[f] = part[:, b * width:(b + 1) * width]

            @pl.when(me != f)
            def _():
                block_copy(rsend, rrecv, rs_sem, rr_sem, f, me).start()

    rrecv[me] = rsend[me]
    wait_block(rsend, rrecv, rs_sem, rr_sem)
    for f in range(n):
        ret_t[:, f * width:(f + 1) * width] = rrecv[f]

    def finish(c, carry):
        span = pl.ds(pl.multiple_of(c * chunk, chunk), chunk)
        part = jnp.dot(ret_t[...], atab[:, span], preferred_element_type=f32)
        out[span, :] = part.T
        return carry

    lax.fori_loop(0, rows_total // chunk, finish, 0)

    def sent_vis(d, carry):
        vis_copy(lax.rem(flat + d, devices), flat).wait_send()
        return carry

    lax.fori_loop(1, devices, sent_vis, 0)

    def sent_blocks(d, carry):
        to = lax.rem(me + d, n)
        block_copy(csend, crecv, cs_sem, cr_sem, to, me).wait_send()
        block_copy(rsend, rrecv, rs_sem, rr_sem, to, me).wait_send()
        return carry

    lax.fori_loop(1, n, sent_blocks, 0)


def solution(mesh):
    n, ncol = mesh.shape["facet"], mesh.shape["col"]
    devices = n * ncol

    def per_device(strips, offsets, vis_subgrid, vis_uv, observed, weights):
        rows_total, width = strips.shape
        nvis = vis_subgrid.shape[0]
        cap = 2 * nvis // devices
        quarter = n // 4
        total = devices * cap
        cas, dif, taper = cas_tables(rows_total, width)
        ctab, cplace = grid_tables(quarter, width, SG)
        f32, bf16 = jnp.float32, jnp.bfloat16
        return pl.pallas_call(
            functools.partial(kernel, n, ncol, cap),
            out_shape=jax.ShapeDtypeStruct((rows_total, width), f32),
            in_specs=[pl.BlockSpec(memory_space=pltpu.VMEM)] * 11,
            out_specs=pl.BlockSpec(memory_space=pltpu.VMEM),
            scratch_shapes=[
                pltpu.VMEM((n * width, rows_total), bf16),
                pltpu.VMEM((n, 1, rows_total), f32),
                pltpu.VMEM((n, 1, rows_total), f32),
                pltpu.VMEM((devices, VALS, LANES), f32),
                pltpu.VMEM((devices, VALS, LANES), f32),
                pltpu.VMEM((n, width, width), bf16),
                pltpu.VMEM((n, width, width), bf16),
                pltpu.VMEM((n, width, width), bf16),
                pltpu.VMEM((n, width, width), bf16),
                pltpu.VMEM((VALS, total), f32),
                pltpu.VMEM((SG, total), bf16),
                pltpu.VMEM((SG, total), bf16),
                pltpu.VMEM((SG, total), bf16),
                pltpu.VMEM((SG, quarter * width), bf16),
                pltpu.VMEM((SG, SG), bf16),
                pltpu.VMEM((width, n * width), bf16),
                pltpu.SemaphoreType.DMA((devices,)),
                pltpu.SemaphoreType.DMA((devices,)),
                pltpu.SemaphoreType.DMA((n,)),
                pltpu.SemaphoreType.DMA((n,)),
                pltpu.SemaphoreType.DMA((n,)),
                pltpu.SemaphoreType.DMA((n,)),
            ],
            compiler_params=pltpu.CompilerParams(
                collective_id=0, has_side_effects=True, vmem_limit_bytes=58 * 1024 * 1024
            ),
        )(
            strips, offsets.reshape(n, 1), vis_subgrid.reshape(1, nvis),
            vis_uv.reshape(1, nvis), observed.reshape(1, nvis), weights.reshape(1, nvis),
            jnp.asarray(cas), jnp.asarray(dif), jnp.asarray(taper),
            jnp.asarray(ctab), jnp.asarray(cplace),
        )

    in_specs = (
        P("facet", "col"),
        P("col", None),
        P(("facet", "col")),
        P(("facet", "col")),
        P(("facet", "col")),
        P(("facet", "col")),
    )
    return jax.shard_map(
        per_device, mesh=mesh, in_specs=in_specs, out_specs=P("facet", "col"), check_vma=False
    )
```

```python
import functools
import math

import jax
import jax.numpy as jnp
import numpy as np
from jax import lax
from jax.experimental import pallas as pl
from jax.experimental.pallas import tpu as pltpu
from jax.sharding import PartitionSpec as P

SG = 512
LANES = 128
VALS = 8


def cas_tables(rows_total, width):
    phase = np.arange(width)[:, None] * np.arange(rows_total)[None, :] % rows_total
    angle = 2.0 * np.pi * phase / rows_total
    taper = (0.6 - 0.4 * np.cos(2.0 * np.pi * np.arange(rows_total) / rows_total)) / math.sqrt(
        rows_total
    )
    cas = (np.cos(angle) + np.sin(angle)).astype(np.float32)
    dif = (np.cos(angle) - np.sin(angle)).astype(np.float32)
    return cas, dif, taper.astype(np.float32)[None, :]


def grid_tables(quarter, width, sub_size):
    phase = np.arange(sub_size)[:, None] * np.arange(sub_size)[None, :] % sub_size
    angle = 2.0 * np.pi * phase / sub_size
    cas = ((np.cos(angle) + np.sin(angle)) / math.sqrt(sub_size)).astype(jnp.bfloat16)
    start = np.arange(quarter) * sub_size // quarter
    target = (start[:, None] + np.arange(width)[None, :]).reshape(-1) % sub_size
    return cas, cas[target]


def sin_cos(turn):
    quad = jnp.floor(4.0 * turn + 0.5)
    x = (turn - 0.25 * quad) * (2.0 * math.pi)
    y = x * x
    s = x * (1.0 + y * (-1.0 / 6 + y * (1.0 / 120 + y * (-1.0 / 5040 + y * (1.0 / 362880)))))
    c = 1.0 + y * (-0.5 + y * (1.0 / 24 + y * (-1.0 / 720 + y * (1.0 / 40320))))
    one, two, three = quad == 1.0, quad == 2.0, quad == 3.0
    sine = jnp.where(one, c, jnp.where(two, -s, jnp.where(three, -c, s)))
    cosine = jnp.where(one, -s, jnp.where(two, -c, jnp.where(three, s, c)))
    return sine, cosine


def kernel(
    n, ncol, cap,
    strips, offs, vsub, vuv, obs, wts, cas, dif, taper, ctab, cplace,
    a_out, ret_t,
    atab, cos_rows, sin_rows, vsend, vrecv, csend, crecv, rsend, rrecv,
    vis, hot_u, hot_v, hot_w, grid_s, grid_f,
    vs_sem, vr_sem, cs_sem, cr_sem, rs_sem, rr_sem, a_sem,
):
    rows_total, width = strips.shape
    devices = n * ncol
    quarter = n // 4
    nvis = vsub.shape[1]
    group = LANES // cap
    groups = devices // group
    me = lax.axis_index("facet")
    my_col = lax.axis_index("col")
    flat = me * ncol + my_col
    f32, bf16 = jnp.float32, jnp.bfloat16

    barrier = pltpu.get_barrier_semaphore()

    def greet(d, carry):
        t = lax.rem(flat + d, devices)
        pl.semaphore_signal(
            barrier, inc=1, device_id={"facet": t // ncol, "col": lax.rem(t, ncol)},
            device_id_type=pl.DeviceIdType.MESH,
        )
        return carry

    lax.fori_loop(1, devices, greet, 0)

    sub = vsub[...]
    hits = lax.broadcasted_iota(jnp.int32, (devices, nvis), 0) == sub
    hits_f = jnp.where(hits, 1.0, 0.0).astype(f32)
    before = (
        lax.broadcasted_iota(jnp.int32, (nvis, nvis), 0)
        < lax.broadcasted_iota(jnp.int32, (nvis, nvis), 1)
    )
    before = jnp.where(before, 1.0, 0.0).astype(bf16)
    counts = jnp.dot(hits_f.astype(bf16), before, preferred_element_type=f32)
    rank = jnp.sum(counts * hits_f, axis=0, keepdims=True)
    lane = rank + (lax.rem(flat, group) * cap).astype(f32)
    slots = lax.broadcasted_iota(jnp.int32, (LANES, nvis), 0).astype(f32) == lane
    slots = jnp.where(slots, 1.0, 0.0).astype(f32)
    uv = vuv[...]
    pu = (uv // SG).astype(f32)
    pv = (uv % SG).astype(f32)
    vals = jnp.concatenate(
        [pu, pv, obs[...], wts[...], jnp.zeros((VALS - 4, nvis), f32)], axis=0
    )
    left = hits_f[:, None, :] * vals[None, :, :]
    packed = lax.dot_general(
        left.reshape(devices * VALS, nvis), slots, (((1,), (1,)), ((), ())),
        precision=lax.Precision.HIGHEST, preferred_element_type=f32,
    )
    vsend[...] = packed.reshape(devices, VALS, LANES)
    vrecv[flat] = vsend[flat]

    row = lax.broadcasted_iota(jnp.int32, (n, rows_total), 1)
    same = (
        lax.broadcasted_iota(jnp.int32, (n, n), 0) == lax.broadcasted_iota(jnp.int32, (n, n), 1)
    )
    shift = jnp.sum(jnp.where(same, offs[...], 0).astype(f32), axis=1, keepdims=True)
    turn = ((shift.astype(jnp.int32) * row) % rows_total).astype(f32) * (1.0 / rows_total)
    sine, cosine = sin_cos(turn)
    cos_rows[...] = (cosine * taper[...]).reshape(n, 1, rows_total)
    sin_rows[...] = (sine * taper[...]).reshape(n, 1, rows_total)

    pl.semaphore_wait(barrier, devices - 1)

    def vis_copy(to, source):
        return pltpu.make_async_remote_copy(
            src_ref=vsend.at[to], dst_ref=vrecv.at[source],
            send_sem=vs_sem.at[to], recv_sem=vr_sem.at[source],
            device_id={"facet": to // ncol, "col": lax.rem(to, ncol)},
            device_id_type=pl.DeviceIdType.MESH,
        )

    def block_copy(send, recv, s_sem, r_sem, to, source):
        return pltpu.make_async_remote_copy(
            src_ref=send.at[to], dst_ref=recv.at[source],
            send_sem=s_sem.at[to], recv_sem=r_sem.at[source],
            device_id={"facet": to}, device_id_type=pl.DeviceIdType.MESH,
        )

    def send_vis(d, carry):
        vis_copy(lax.rem(flat + d, devices), flat).start()
        return carry

    lax.fori_loop(1, devices, send_vis, 0)

    chunk = min(512, rows_total)

    def table_copy(i):
        o = lax.rem(me + 1 + i, n)
        at = pl.ds(pl.multiple_of(o * width, width), width)
        return pltpu.make_async_copy(atab.at[lax.rem(i, 2)], a_out.at[at], a_sem.at[o])

    def one_owner(i, carry):
        o = lax.rem(me + 1 + i, n)
        slot = lax.rem(i, 2)

        @pl.when(i >= 2)
        def _():
            table_copy(i - 2).wait()

        acc = jnp.zeros((width, strips.shape[1]), f32)
        for c in range(rows_total // chunk):
            cols = pl.ds(c * chunk, chunk)
            mixed = cos_rows[o, :, cols] * cas[:, cols] + sin_rows[o, :, cols] * dif[:, cols]
            mixed = mixed.astype(bf16)
            atab[slot, :, cols] = mixed
            acc = acc + jnp.dot(mixed, strips[cols, :], preferred_element_type=f32)
        csend[o] = acc.astype(bf16)
        table_copy(i).start()

        @pl.when(i < n - 1)
        def _():
            block_copy(csend, crecv, cs_sem, cr_sem, o, me).start()

        return carry

    lax.fori_loop(0, n, one_owner, 0)
    crecv[me] = csend[me]

    def wait_vis(d, carry):
        vis_copy(flat, lax.rem(flat + d, devices)).wait_recv()
        return carry

    lax.fori_loop(1, devices, wait_vis, 0)
    for g in range(groups):
        vis[:, g * LANES:(g + 1) * LANES] = jnp.sum(vrecv[g * group:(g + 1) * group], axis=0)
    total = groups * LANES
    step = min(256, total)
    pixel = lax.broadcasted_iota(jnp.int32, (SG, step), 0).astype(f32)
    for v in range(total // step):
        span = slice(v * step, (v + 1) * step)
        hot_u[:, span] = jnp.where(pixel == vis[0:1, span], 1.0, 0.0).astype(bf16)
        hot_v[:, span] = jnp.where(pixel == vis[1:2, span], 1.0, 0.0).astype(bf16)

    def wait_block(send, recv, s_sem, r_sem):
        def body(d, carry):
            block_copy(send, recv, s_sem, r_sem, me, lax.rem(me + n - d, n)).wait_recv()
            return carry

        lax.fori_loop(1, n, body, 0)

    wait_block(csend, crecv, cs_sem, cr_sem)
    for f in range(n):
        q, b = f // 4, f % 4
        grid_s[b * width:(b + 1) * width, q * width:(q + 1) * width] = crecv[f]
    half = jnp.dot(ctab[...], grid_s[...], preferred_element_type=f32).astype(bf16)
    grid_f[...] = jnp.dot(half, cplace[...], preferred_element_type=f32).astype(bf16)

    def residual(v, carry):
        span = pl.ds(pl.multiple_of(v * step, step), step)
        rows = jnp.dot(grid_f[...], hot_v[:, span], preferred_element_type=f32)
        predicted = jnp.sum(rows * hot_u[:, span].astype(f32), axis=0, keepdims=True)
        weighted = vis[3:4, span] * (vis[2:3, span] - predicted)
        hot_w[:, span] = (hot_v[:, span].astype(f32) * weighted).astype(bf16)
        return carry

    lax.fori_loop(0, total // step, residual, 0)
    weight_t = lax.dot_general(
        hot_w[...], hot_u[...], (((1,), (1,)), ((), ())), preferred_element_type=f32
    ).astype(bf16)
    grid_g = jnp.dot(weight_t, ctab[...], preferred_element_type=f32).astype(bf16)
    for q in range(quarter):
        part = jnp.dot(
            cplace[q * width:(q + 1) * width, :], grid_g, preferred_element_type=f32
        )
        part = (part * math.sqrt(SG)).astype(bf16)
        for b in range(4):
            f = q * 4 + b
            rsend[f] = part[:, b * width:(b + 1) * width]

            @pl.when(me != f)
            def _():
                block_copy(rsend, rrecv, rs_sem, rr_sem, f, me).start()

    rrecv[me] = rsend[me]
    wait_block(rsend, rrecv, rs_sem, rr_sem)
    for f in range(n):
        ret_t[:, f * width:(f + 1) * width] = rrecv[f]

    table_copy(n - 2).wait()
    table_copy(n - 1).wait()

    def sent_vis(d, carry):
        vis_copy(lax.rem(flat + d, devices), flat).wait_send()
        return carry

    lax.fori_loop(1, devices, sent_vis, 0)

    def sent_blocks(d, carry):
        to = lax.rem(me + d, n)
        block_copy(csend, crecv, cs_sem, cr_sem, to, me).wait_send()
        block_copy(rsend, rrecv, rs_sem, rr_sem, to, me).wait_send()
        return carry

    lax.fori_loop(1, n, sent_blocks, 0)


def finish(ret_t, atab, out):
    out[...] = jnp.dot(ret_t[...], atab[...], preferred_element_type=jnp.float32).T


def solution(mesh):
    n, ncol = mesh.shape["facet"], mesh.shape["col"]
    devices = n * ncol

    def per_device(strips, offsets, vis_subgrid, vis_uv, observed, weights):
        rows_total, width = strips.shape
        nvis = vis_subgrid.shape[0]
        cap = 2 * nvis // devices
        quarter = n // 4
        total = devices * cap
        cas, dif, taper = cas_tables(rows_total, width)
        ctab, cplace = grid_tables(quarter, width, SG)
        f32, bf16 = jnp.float32, jnp.bfloat16
        tables, returned = pl.pallas_call(
            functools.partial(kernel, n, ncol, cap),
            out_shape=(
                jax.ShapeDtypeStruct((n * width, rows_total), bf16),
                jax.ShapeDtypeStruct((width, n * width), bf16),
            ),
            in_specs=[pl.BlockSpec(memory_space=pltpu.VMEM)] * 11,
            out_specs=(
                pl.BlockSpec(memory_space=pl.ANY), pl.BlockSpec(memory_space=pltpu.VMEM)
            ),
            scratch_shapes=[
                pltpu.VMEM((2, width, rows_total), bf16),
                pltpu.VMEM((n, 1, rows_total), f32),
                pltpu.VMEM((n, 1, rows_total), f32),
                pltpu.VMEM((devices, VALS, LANES), f32),
                pltpu.VMEM((devices, VALS, LANES), f32),
                pltpu.VMEM((n, width, width), bf16),
                pltpu.VMEM((n, width, width), bf16),
                pltpu.VMEM((n, width, width), bf16),
                pltpu.VMEM((n, width, width), bf16),
                pltpu.VMEM((VALS, total), f32),
                pltpu.VMEM((SG, total), bf16),
                pltpu.VMEM((SG, total), bf16),
                pltpu.VMEM((SG, total), bf16),
                pltpu.VMEM((SG, quarter * width), bf16),
                pltpu.VMEM((SG, SG), bf16),
                pltpu.SemaphoreType.DMA((devices,)),
                pltpu.SemaphoreType.DMA((devices,)),
                pltpu.SemaphoreType.DMA((n,)),
                pltpu.SemaphoreType.DMA((n,)),
                pltpu.SemaphoreType.DMA((n,)),
                pltpu.SemaphoreType.DMA((n,)),
                pltpu.SemaphoreType.DMA((n,)),
            ],
            compiler_params=pltpu.CompilerParams(
                collective_id=0, has_side_effects=True, vmem_limit_bytes=36 * 1024 * 1024
            ),
        )(
            strips, offsets, vis_subgrid.reshape(1, nvis),
            vis_uv.reshape(1, nvis), observed.reshape(1, nvis), weights.reshape(1, nvis),
            jnp.asarray(cas), jnp.asarray(dif), jnp.asarray(taper),
            jnp.asarray(ctab), jnp.asarray(cplace),
        )
        chunk = min(512, rows_total)
        return pl.pallas_call(
            finish,
            out_shape=jax.ShapeDtypeStruct((rows_total, width), f32),
            grid=(rows_total // chunk,),
            in_specs=[
                pl.BlockSpec((width, n * width), lambda i: (0, 0)),
                pl.BlockSpec((n * width, chunk), lambda i: (0, i)),
            ],
            out_specs=pl.BlockSpec((chunk, width), lambda i: (i, 0)),
            compiler_params=pltpu.CompilerParams(vmem_limit_bytes=20 * 1024 * 1024),
        )(returned, tables)

    in_specs = (
        P("facet", "col"),
        P("col", None),
        P(("facet", "col")),
        P(("facet", "col")),
        P(("facet", "col")),
        P(("facet", "col")),
    )
    return jax.shard_map(
        per_device, mesh=mesh, in_specs=in_specs, out_specs=P("facet", "col"), check_vma=False
    )
```

```python
import functools
import math

import jax
import jax.numpy as jnp
import numpy as np
from jax import lax
from jax.experimental import pallas as pl
from jax.experimental.pallas import tpu as pltpu
from jax.sharding import PartitionSpec as P

SG = 512
LANES = 128
VALS = 8


def cas_tables(rows_total, width):
    phase = np.arange(width)[:, None] * np.arange(rows_total)[None, :] % rows_total
    angle = 2.0 * np.pi * phase / rows_total
    taper = (0.6 - 0.4 * np.cos(2.0 * np.pi * np.arange(rows_total) / rows_total)) / math.sqrt(
        rows_total
    )
    cas = (np.cos(angle) + np.sin(angle)).astype(np.float32)
    dif = (np.cos(angle) - np.sin(angle)).astype(np.float32)
    return cas, dif, taper.astype(np.float32)[None, :]


def grid_tables(quarter, width, sub_size):
    phase = np.arange(sub_size)[:, None] * np.arange(sub_size)[None, :] % sub_size
    angle = 2.0 * np.pi * phase / sub_size
    cas = ((np.cos(angle) + np.sin(angle)) / math.sqrt(sub_size)).astype(jnp.bfloat16)
    start = np.arange(quarter) * sub_size // quarter
    target = (start[:, None] + np.arange(width)[None, :]).reshape(-1) % sub_size
    return cas, cas[target]


def sin_cos(turn):
    quad = jnp.floor(4.0 * turn + 0.5)
    x = (turn - 0.25 * quad) * (2.0 * math.pi)
    y = x * x
    s = x * (1.0 + y * (-1.0 / 6 + y * (1.0 / 120 + y * (-1.0 / 5040 + y * (1.0 / 362880)))))
    c = 1.0 + y * (-0.5 + y * (1.0 / 24 + y * (-1.0 / 720 + y * (1.0 / 40320))))
    one, two, three = quad == 1.0, quad == 2.0, quad == 3.0
    sine = jnp.where(one, c, jnp.where(two, -s, jnp.where(three, -c, s)))
    cosine = jnp.where(one, -s, jnp.where(two, -c, jnp.where(three, s, c)))
    return sine, cosine


def kernel(
    n, ncol, cap,
    strips_in, offs_in, vsub_in, vuv_in, obs_in, wts_in, cas_in, dif_in, taper_in, ctab_in,
    cplace_in,
    a_out, ret_t,
    atab, cos_rows, sin_rows, vsend, vrecv, csend, crecv, rsend, rrecv,
    vis, hot_u, hot_v, hot_w, grid_s, grid_f,
    vs_sem, vr_sem, cs_sem, cr_sem, rs_sem, rr_sem, a_sem,
    strips, offs, vsub, vuv, obs, wts, cas, dif, taper, ctab, cplace, in_sem,
):
    rows_total, width = strips.shape
    devices = n * ncol
    quarter = n // 4
    nvis = vsub.shape[1]
    group = LANES // cap
    groups = devices // group
    me = lax.axis_index("facet")
    my_col = lax.axis_index("col")
    flat = me * ncol + my_col
    f32, bf16 = jnp.float32, jnp.bfloat16

    loads = [
        pltpu.make_async_copy(source, held, in_sem.at[at])
        for at, (source, held) in enumerate([
            (vsub_in, vsub), (vuv_in, vuv), (obs_in, obs), (wts_in, wts), (offs_in, offs),
            (taper_in, taper), (cas_in, cas), (dif_in, dif), (strips_in, strips),
            (ctab_in, ctab), (cplace_in, cplace),
        ])
    ]
    for load in loads:
        load.start()

    barrier = pltpu.get_barrier_semaphore()

    def greet(d, carry):
        t = lax.rem(flat + d, devices)
        pl.semaphore_signal(
            barrier, inc=1, device_id={"facet": t // ncol, "col": lax.rem(t, ncol)},
            device_id_type=pl.DeviceIdType.MESH,
        )
        return carry

    lax.fori_loop(1, devices, greet, 0)

    for load in loads[:4]:
        load.wait()
    sub = vsub[...]
    hits = lax.broadcasted_iota(jnp.int32, (devices, nvis), 0) == sub
    hits_f = jnp.where(hits, 1.0, 0.0).astype(f32)
    before = (
        lax.broadcasted_iota(jnp.int32, (nvis, nvis), 0)
        < lax.broadcasted_iota(jnp.int32, (nvis, nvis), 1)
    )
    before = jnp.where(before, 1.0, 0.0).astype(bf16)
    counts = jnp.dot(hits_f.astype(bf16), before, preferred_element_type=f32)
    rank = jnp.sum(counts * hits_f, axis=0, keepdims=True)
    lane = rank + (lax.rem(flat, group) * cap).astype(f32)
    slots = lax.broadcasted_iota(jnp.int32, (LANES, nvis), 0).astype(f32) == lane
    slots = jnp.where(slots, 1.0, 0.0).astype(f32)
    uv = vuv[...]
    pu = (uv // SG).astype(f32)
    pv = (uv % SG).astype(f32)
    vals = jnp.concatenate(
        [pu, pv, obs[...], wts[...], jnp.zeros((VALS - 4, nvis), f32)], axis=0
    )
    left = hits_f[:, None, :] * vals[None, :, :]
    packed = lax.dot_general(
        left.reshape(devices * VALS, nvis), slots, (((1,), (1,)), ((), ())),
        precision=lax.Precision.HIGHEST, preferred_element_type=f32,
    )
    vsend[...] = packed.reshape(devices, VALS, LANES)
    vrecv[flat] = vsend[flat]

    for load in loads[4:6]:
        load.wait()
    row = lax.broadcasted_iota(jnp.int32, (n, rows_total), 1)
    same = (
        lax.broadcasted_iota(jnp.int32, (n, n), 0) == lax.broadcasted_iota(jnp.int32, (n, n), 1)
    )
    shift = jnp.sum(jnp.where(same, offs[...], 0).astype(f32), axis=1, keepdims=True)
    turn = ((shift.astype(jnp.int32) * row) % rows_total).astype(f32) * (1.0 / rows_total)
    sine, cosine = sin_cos(turn)
    cos_rows[...] = (cosine * taper[...]).reshape(n, 1, rows_total)
    sin_rows[...] = (sine * taper[...]).reshape(n, 1, rows_total)

    pl.semaphore_wait(barrier, devices - 1)

    def vis_copy(to, source):
        return pltpu.make_async_remote_copy(
            src_ref=vsend.at[to], dst_ref=vrecv.at[source],
            send_sem=vs_sem.at[to], recv_sem=vr_sem.at[source],
            device_id={"facet": to // ncol, "col": lax.rem(to, ncol)},
            device_id_type=pl.DeviceIdType.MESH,
        )

    def block_copy(send, recv, s_sem, r_sem, to, source):
        return pltpu.make_async_remote_copy(
            src_ref=send.at[to], dst_ref=recv.at[source],
            send_sem=s_sem.at[to], recv_sem=r_sem.at[source],
            device_id={"facet": to}, device_id_type=pl.DeviceIdType.MESH,
        )

    def send_vis(d, carry):
        vis_copy(lax.rem(flat + d, devices), flat).start()
        return carry

    lax.fori_loop(1, devices, send_vis, 0)

    for load in loads[6:9]:
        load.wait()
    chunk = min(512, rows_total)

    def table_copy(i):
        o = lax.rem(me + 1 + i, n)
        at = pl.ds(pl.multiple_of(o * width, width), width)
        return pltpu.make_async_copy(atab.at[lax.rem(i, 2)], a_out.at[at], a_sem.at[o])

    def one_owner(i, carry):
        o = lax.rem(me + 1 + i, n)
        slot = lax.rem(i, 2)

        @pl.when(i >= 2)
        def _():
            table_copy(i - 2).wait()

        acc = jnp.zeros((width, strips.shape[1]), f32)
        for c in range(rows_total // chunk):
            cols = pl.ds(c * chunk, chunk)
            mixed = cos_rows[o, :, cols] * cas[:, cols] + sin_rows[o, :, cols] * dif[:, cols]
            mixed = mixed.astype(bf16)
            atab[slot, :, cols] = mixed
            acc = acc + jnp.dot(mixed, strips[cols, :], preferred_element_type=f32)
        csend[o] = acc.astype(bf16)
        table_copy(i).start()

        @pl.when(i < n - 1)
        def _():
            block_copy(csend, crecv, cs_sem, cr_sem, o, me).start()

        return carry

    lax.fori_loop(0, n, one_owner, 0)
    crecv[me] = csend[me]

    def wait_vis(d, carry):
        vis_copy(flat, lax.rem(flat + d, devices)).wait_recv()
        return carry

    lax.fori_loop(1, devices, wait_vis, 0)
    for g in range(groups):
        vis[:, g * LANES:(g + 1) * LANES] = jnp.sum(vrecv[g * group:(g + 1) * group], axis=0)
    total = groups * LANES
    step = min(256, total)
    pixel = lax.broadcasted_iota(jnp.int32, (SG, step), 0).astype(f32)
    for v in range(total // step):
        span = slice(v * step, (v + 1) * step)
        hot_u[:, span] = jnp.where(pixel == vis[0:1, span], 1.0, 0.0).astype(bf16)
        hot_v[:, span] = jnp.where(pixel == vis[1:2, span], 1.0, 0.0).astype(bf16)

    def wait_block(send, recv, s_sem, r_sem):
        def body(d, carry):
            block_copy(send, recv, s_sem, r_sem, me, lax.rem(me + n - d, n)).wait_recv()
            return carry

        lax.fori_loop(1, n, body, 0)

    for load in loads[9:]:
        load.wait()
    wait_block(csend, crecv, cs_sem, cr_sem)
    for f in range(n):
        q, b = f // 4, f % 4
        grid_s[b * width:(b + 1) * width, q * width:(q + 1) * width] = crecv[f]
    half = jnp.dot(ctab[...], grid_s[...], preferred_element_type=f32).astype(bf16)
    grid_f[...] = jnp.dot(half, cplace[...], preferred_element_type=f32).astype(bf16)

    def residual(v, carry):
        span = pl.ds(pl.multiple_of(v * step, step), step)
        rows = jnp.dot(grid_f[...], hot_v[:, span], preferred_element_type=f32)
        predicted = jnp.sum(rows * hot_u[:, span].astype(f32), axis=0, keepdims=True)
        weighted = vis[3:4, span] * (vis[2:3, span] - predicted)
        hot_w[:, span] = (hot_v[:, span].astype(f32) * weighted).astype(bf16)
        return carry

    lax.fori_loop(0, total // step, residual, 0)
    weight_t = lax.dot_general(
        hot_w[...], hot_u[...], (((1,), (1,)), ((), ())), preferred_element_type=f32
    ).astype(bf16)
    grid_g = jnp.dot(weight_t, ctab[...], preferred_element_type=f32).astype(bf16)
    for q in range(quarter):
        part = jnp.dot(
            cplace[q * width:(q + 1) * width, :], grid_g, preferred_element_type=f32
        )
        part = (part * math.sqrt(SG)).astype(bf16)
        for b in range(4):
            f = q * 4 + b
            rsend[f] = part[:, b * width:(b + 1) * width]

            @pl.when(me != f)
            def _():
                block_copy(rsend, rrecv, rs_sem, rr_sem, f, me).start()

    rrecv[me] = rsend[me]
    wait_block(rsend, rrecv, rs_sem, rr_sem)
    for f in range(n):
        ret_t[:, f * width:(f + 1) * width] = rrecv[f]

    table_copy(n - 2).wait()
    table_copy(n - 1).wait()

    def sent_vis(d, carry):
        vis_copy(lax.rem(flat + d, devices), flat).wait_send()
        return carry

    lax.fori_loop(1, devices, sent_vis, 0)

    def sent_blocks(d, carry):
        to = lax.rem(me + d, n)
        block_copy(csend, crecv, cs_sem, cr_sem, to, me).wait_send()
        block_copy(rsend, rrecv, rs_sem, rr_sem, to, me).wait_send()
        return carry

    lax.fori_loop(1, n, sent_blocks, 0)


def finish(ret_t, atab, out):
    out[...] = jnp.dot(ret_t[...], atab[...], preferred_element_type=jnp.float32).T


def solution(mesh):
    n, ncol = mesh.shape["facet"], mesh.shape["col"]
    devices = n * ncol

    def per_device(strips, offsets, vis_subgrid, vis_uv, observed, weights):
        rows_total, width = strips.shape
        nvis = vis_subgrid.shape[0]
        cap = 2 * nvis // devices
        quarter = n // 4
        total = devices * cap
        cas, dif, taper = cas_tables(rows_total, width)
        ctab, cplace = grid_tables(quarter, width, SG)
        f32, bf16 = jnp.float32, jnp.bfloat16
        tables, returned = pl.pallas_call(
            functools.partial(kernel, n, ncol, cap),
            out_shape=(
                jax.ShapeDtypeStruct((n * width, rows_total), bf16),
                jax.ShapeDtypeStruct((width, n * width), bf16),
            ),
            in_specs=[pl.BlockSpec(memory_space=pl.ANY)] * 11,
            out_specs=(
                pl.BlockSpec(memory_space=pl.ANY), pl.BlockSpec(memory_space=pltpu.VMEM)
            ),
            scratch_shapes=[
                pltpu.VMEM((2, width, rows_total), bf16),
                pltpu.VMEM((n, 1, rows_total), f32),
                pltpu.VMEM((n, 1, rows_total), f32),
                pltpu.VMEM((devices, VALS, LANES), f32),
                pltpu.VMEM((devices, VALS, LANES), f32),
                pltpu.VMEM((n, width, width), bf16),
                pltpu.VMEM((n, width, width), bf16),
                pltpu.VMEM((n, width, width), bf16),
                pltpu.VMEM((n, width, width), bf16),
                pltpu.VMEM((VALS, total), f32),
                pltpu.VMEM((SG, total), bf16),
                pltpu.VMEM((SG, total), bf16),
                pltpu.VMEM((SG, total), bf16),
                pltpu.VMEM((SG, quarter * width), bf16),
                pltpu.VMEM((SG, SG), bf16),
                pltpu.SemaphoreType.DMA((devices,)),
                pltpu.SemaphoreType.DMA((devices,)),
                pltpu.SemaphoreType.DMA((n,)),
                pltpu.SemaphoreType.DMA((n,)),
                pltpu.SemaphoreType.DMA((n,)),
                pltpu.SemaphoreType.DMA((n,)),
                pltpu.SemaphoreType.DMA((n,)),
                pltpu.VMEM((rows_total, width), bf16),
                pltpu.VMEM((1, n), jnp.int32),
                pltpu.VMEM((1, nvis), jnp.int32),
                pltpu.VMEM((1, nvis), jnp.int32),
                pltpu.VMEM((1, nvis), f32),
                pltpu.VMEM((1, nvis), f32),
                pltpu.VMEM((width, rows_total), f32),
                pltpu.VMEM((width, rows_total), f32),
                pltpu.VMEM((1, rows_total), f32),
                pltpu.VMEM((SG, SG), bf16),
                pltpu.VMEM((quarter * width, SG), bf16),
                pltpu.SemaphoreType.DMA((11,)),
            ],
            compiler_params=pltpu.CompilerParams(
                collective_id=0, has_side_effects=True, vmem_limit_bytes=58 * 1024 * 1024
            ),
        )(
            strips, offsets, vis_subgrid.reshape(1, nvis),
            vis_uv.reshape(1, nvis), observed.reshape(1, nvis), weights.reshape(1, nvis),
            jnp.asarray(cas), jnp.asarray(dif), jnp.asarray(taper),
            jnp.asarray(ctab), jnp.asarray(cplace),
        )
        chunk = min(1024, rows_total)
        return pl.pallas_call(
            finish,
            out_shape=jax.ShapeDtypeStruct((rows_total, width), f32),
            grid=(rows_total // chunk,),
            in_specs=[
                pl.BlockSpec((width, n * width), lambda i: (0, 0)),
                pl.BlockSpec((n * width, chunk), lambda i: (0, i)),
            ],
            out_specs=pl.BlockSpec((chunk, width), lambda i: (i, 0)),
            compiler_params=pltpu.CompilerParams(vmem_limit_bytes=58 * 1024 * 1024),
        )(returned, tables)

    in_specs = (
        P("facet", "col"),
        P("col", None),
        P(("facet", "col")),
        P(("facet", "col")),
        P(("facet", "col")),
        P(("facet", "col")),
    )
    return jax.shard_map(
        per_device, mesh=mesh, in_specs=in_specs, out_specs=P("facet", "col"), check_vma=False
    )
```

```python
import functools
import math

import jax
import jax.numpy as jnp
import numpy as np
from jax import lax
from jax.experimental import pallas as pl
from jax.experimental.pallas import tpu as pltpu
from jax.sharding import PartitionSpec as P

SG = 512
LANES = 128
VALS = 8


def cas_tables(rows_total, width):
    phase = np.arange(width)[:, None] * np.arange(rows_total)[None, :] % rows_total
    angle = 2.0 * np.pi * phase / rows_total
    taper = (0.6 - 0.4 * np.cos(2.0 * np.pi * np.arange(rows_total) / rows_total)) / math.sqrt(
        rows_total
    )
    cas = (np.cos(angle) + np.sin(angle)).astype(np.float32)
    dif = (np.cos(angle) - np.sin(angle)).astype(np.float32)
    return cas, dif, taper.astype(np.float32)[None, :]


def grid_tables(quarter, width, sub_size):
    phase = np.arange(sub_size)[:, None] * np.arange(sub_size)[None, :] % sub_size
    angle = 2.0 * np.pi * phase / sub_size
    cas = ((np.cos(angle) + np.sin(angle)) / math.sqrt(sub_size)).astype(jnp.bfloat16)
    start = np.arange(quarter) * sub_size // quarter
    target = (start[:, None] + np.arange(width)[None, :]).reshape(-1) % sub_size
    return cas, cas[target]


def sin_cos(turn):
    quad = jnp.floor(4.0 * turn + 0.5)
    x = (turn - 0.25 * quad) * (2.0 * math.pi)
    y = x * x
    s = x * (1.0 + y * (-1.0 / 6 + y * (1.0 / 120 + y * (-1.0 / 5040 + y * (1.0 / 362880)))))
    c = 1.0 + y * (-0.5 + y * (1.0 / 24 + y * (-1.0 / 720 + y * (1.0 / 40320))))
    one, two, three = quad == 1.0, quad == 2.0, quad == 3.0
    sine = jnp.where(one, c, jnp.where(two, -s, jnp.where(three, -c, s)))
    cosine = jnp.where(one, -s, jnp.where(two, -c, jnp.where(three, s, c)))
    return sine, cosine


def kernel(
    n, ncol, cap,
    strips_in, offs_in, vsub_in, vuv_in, obs_in, wts_in, cas_in, dif_in, taper_in, ctab_in,
    cplace_in,
    a_out, ret_t,
    atab, cos_rows, sin_rows, vsend, vrecv, csend, crecv, rsend, rrecv,
    vis, hot_u, hot_v, hot_w, grid_s, grid_f,
    vs_sem, vr_sem, cs_sem, cr_sem, rs_sem, rr_sem, a_sem,
    strips, offs, vsub, vuv, obs, wts, cas, dif, taper, ctab, cplace, in_sem,
):
    rows_total, width = strips.shape
    devices = n * ncol
    quarter = n // 4
    nvis = vsub.shape[1]
    group = LANES // cap
    groups = devices // group
    me = lax.axis_index("facet")
    my_col = lax.axis_index("col")
    flat = me * ncol + my_col
    f32, bf16 = jnp.float32, jnp.bfloat16

    loads = [
        pltpu.make_async_copy(source, held, in_sem.at[at])
        for at, (source, held) in enumerate([
            (vsub_in, vsub), (vuv_in, vuv), (obs_in, obs), (wts_in, wts), (offs_in, offs),
            (taper_in, taper), (cas_in, cas), (dif_in, dif), (strips_in, strips),
            (ctab_in, ctab), (cplace_in, cplace),
        ])
    ]
    for load in loads:
        load.start()

    barrier = pltpu.get_barrier_semaphore()

    def greet(d, carry):
        t = lax.rem(flat + d, devices)
        pl.semaphore_signal(
            barrier, inc=1, device_id={"facet": t // ncol, "col": lax.rem(t, ncol)},
            device_id_type=pl.DeviceIdType.MESH,
        )
        return carry

    lax.fori_loop(1, devices, greet, 0)

    for load in loads[:4]:
        load.wait()
    sub = vsub[...]
    hits = lax.broadcasted_iota(jnp.int32, (devices, nvis), 0) == sub
    hits_f = jnp.where(hits, 1.0, 0.0).astype(f32)
    before = (
        lax.broadcasted_iota(jnp.int32, (nvis, nvis), 0)
        < lax.broadcasted_iota(jnp.int32, (nvis, nvis), 1)
    )
    before = jnp.where(before, 1.0, 0.0).astype(bf16)
    counts = jnp.dot(hits_f.astype(bf16), before, preferred_element_type=f32)
    rank = jnp.sum(counts * hits_f, axis=0, keepdims=True)
    lane = rank + (lax.rem(flat, group) * cap).astype(f32)
    slots = lax.broadcasted_iota(jnp.int32, (LANES, nvis), 0).astype(f32) == lane
    slots = jnp.where(slots, 1.0, 0.0).astype(f32)
    uv = vuv[...]
    pu = (uv // SG).astype(f32)
    pv = (uv % SG).astype(f32)
    vals = jnp.concatenate(
        [pu, pv, obs[...], wts[...], jnp.zeros((VALS - 4, nvis), f32)], axis=0
    )
    left = hits_f[:, None, :] * vals[None, :, :]
    packed = lax.dot_general(
        left.reshape(devices * VALS, nvis), slots, (((1,), (1,)), ((), ())),
        precision=lax.Precision.HIGHEST, preferred_element_type=f32,
    )
    vsend[...] = packed.reshape(devices, VALS, LANES)
    vrecv[flat] = vsend[flat]

    for load in loads[4:6]:
        load.wait()
    row = lax.broadcasted_iota(jnp.int32, (n, rows_total), 1)
    same = (
        lax.broadcasted_iota(jnp.int32, (n, n), 0) == lax.broadcasted_iota(jnp.int32, (n, n), 1)
    )
    shift = jnp.sum(jnp.where(same, offs[...], 0).astype(f32), axis=1, keepdims=True)
    turn = ((shift.astype(jnp.int32) * row) % rows_total).astype(f32) * (1.0 / rows_total)
    sine, cosine = sin_cos(turn)
    cos_rows[...] = (cosine * taper[...]).reshape(n, 1, rows_total)
    sin_rows[...] = (sine * taper[...]).reshape(n, 1, rows_total)

    pl.semaphore_wait(barrier, devices - 1)

    def vis_copy(to, source):
        return pltpu.make_async_remote_copy(
            src_ref=vsend.at[to], dst_ref=vrecv.at[source],
            send_sem=vs_sem.at[to], recv_sem=vr_sem.at[source],
            device_id={"facet": to // ncol, "col": lax.rem(to, ncol)},
            device_id_type=pl.DeviceIdType.MESH,
        )

    def block_copy(send, recv, s_sem, r_sem, to, source):
        return pltpu.make_async_remote_copy(
            src_ref=send.at[to], dst_ref=recv.at[source],
            send_sem=s_sem.at[to], recv_sem=r_sem.at[source],
            device_id={"facet": to}, device_id_type=pl.DeviceIdType.MESH,
        )

    def send_vis(d, carry):
        vis_copy(lax.rem(flat + d, devices), flat).start()
        return carry

    lax.fori_loop(1, devices, send_vis, 0)

    for load in loads[6:9]:
        load.wait()
    chunk = min(512, rows_total)

    def table_copy(i):
        o = lax.rem(me + 1 + i, n)
        at = pl.ds(pl.multiple_of(o * width, width), width)
        return pltpu.make_async_copy(atab.at[lax.rem(i, 2)], a_out.at[at], a_sem.at[o])

    def one_owner(i, carry):
        o = lax.rem(me + 1 + i, n)
        slot = lax.rem(i, 2)

        @pl.when(i >= 2)
        def _():
            table_copy(i - 2).wait()

        acc = jnp.zeros((width, strips.shape[1]), f32)
        for c in range(rows_total // chunk):
            cols = pl.ds(c * chunk, chunk)
            mixed = cos_rows[o, :, cols] * cas[:, cols] + sin_rows[o, :, cols] * dif[:, cols]
            mixed = mixed.astype(bf16)
            atab[slot, :, cols] = mixed
            acc = acc + jnp.dot(mixed, strips[cols, :], preferred_element_type=f32)
        csend[o] = acc.astype(bf16)
        table_copy(i).start()

        @pl.when(i < n - 1)
        def _():
            block_copy(csend, crecv, cs_sem, cr_sem, o, me).start()

        return carry

    lax.fori_loop(0, n, one_owner, 0)
    crecv[me] = csend[me]

    def wait_vis(d, carry):
        vis_copy(flat, lax.rem(flat + d, devices)).wait_recv()
        return carry

    lax.fori_loop(1, devices, wait_vis, 0)
    for g in range(groups):
        vis[:, g * LANES:(g + 1) * LANES] = jnp.sum(vrecv[g * group:(g + 1) * group], axis=0)
    total = groups * LANES
    step = min(256, total)
    pixel = lax.broadcasted_iota(jnp.int32, (SG, step), 0).astype(f32)
    for v in range(total // step):
        span = slice(v * step, (v + 1) * step)
        hot_u[:, span] = jnp.where(pixel == vis[0:1, span], 1.0, 0.0).astype(bf16)
        hot_v[:, span] = jnp.where(pixel == vis[1:2, span], 1.0, 0.0).astype(bf16)

    def wait_block(send, recv, s_sem, r_sem):
        def body(d, carry):
            block_copy(send, recv, s_sem, r_sem, me, lax.rem(me + n - d, n)).wait_recv()
            return carry

        lax.fori_loop(1, n, body, 0)

    for load in loads[9:]:
        load.wait()
    wait_block(csend, crecv, cs_sem, cr_sem)
    for f in range(n):
        q, b = f // 4, f % 4
        grid_s[b * width:(b + 1) * width, q * width:(q + 1) * width] = crecv[f]
    half = jnp.dot(ctab[...], grid_s[...], preferred_element_type=f32).astype(bf16)
    grid_f[...] = jnp.dot(half, cplace[...], preferred_element_type=f32).astype(bf16)

    def residual(v, carry):
        span = pl.ds(pl.multiple_of(v * step, step), step)
        rows = jnp.dot(grid_f[...], hot_v[:, span], preferred_element_type=f32)
        predicted = jnp.sum(rows * hot_u[:, span].astype(f32), axis=0, keepdims=True)
        weighted = vis[3:4, span] * (vis[2:3, span] - predicted)
        hot_w[:, span] = (hot_v[:, span].astype(f32) * weighted).astype(bf16)
        return carry

    lax.fori_loop(0, total // step, residual, 0)
    weight_t = lax.dot_general(
        hot_w[...], hot_u[...], (((1,), (1,)), ((), ())), preferred_element_type=f32
    ).astype(bf16)
    grid_g = jnp.dot(weight_t, ctab[...], preferred_element_type=f32).astype(bf16)
    for q in range(quarter):
        part = jnp.dot(
            cplace[q * width:(q + 1) * width, :], grid_g, preferred_element_type=f32
        )
        part = (part * math.sqrt(SG)).astype(bf16)
        for b in range(4):
            f = q * 4 + b
            rsend[f] = part[:, b * width:(b + 1) * width]

            @pl.when(me != f)
            def _():
                block_copy(rsend, rrecv, rs_sem, rr_sem, f, me).start()

    rrecv[me] = rsend[me]
    wait_block(rsend, rrecv, rs_sem, rr_sem)
    for f in range(n):
        ret_t[:, f * width:(f + 1) * width] = rrecv[f]

    table_copy(n - 2).wait()
    table_copy(n - 1).wait()

    def sent_vis(d, carry):
        vis_copy(lax.rem(flat + d, devices), flat).wait_send()
        return carry

    lax.fori_loop(1, devices, sent_vis, 0)

    def sent_blocks(d, carry):
        to = lax.rem(me + d, n)
        block_copy(csend, crecv, cs_sem, cr_sem, to, me).wait_send()
        block_copy(rsend, rrecv, rs_sem, rr_sem, to, me).wait_send()
        return carry

    lax.fori_loop(1, n, sent_blocks, 0)


def finish(ret_t, atab, out):
    out[...] = jnp.dot(ret_t[...], atab[...], preferred_element_type=jnp.float32).T


def solution(mesh):
    n, ncol = mesh.shape["facet"], mesh.shape["col"]
    devices = n * ncol

    def per_device(strips, offsets, vis_subgrid, vis_uv, observed, weights):
        rows_total, width = strips.shape
        nvis = vis_subgrid.shape[0]
        cap = 2 * nvis // devices
        quarter = n // 4
        total = devices * cap
        cas, dif, taper = cas_tables(rows_total, width)
        ctab, cplace = grid_tables(quarter, width, SG)
        f32, bf16 = jnp.float32, jnp.bfloat16
        tables, returned = pl.pallas_call(
            functools.partial(kernel, n, ncol, cap),
            out_shape=(
                jax.ShapeDtypeStruct((n * width, rows_total), bf16),
                jax.ShapeDtypeStruct((width, n * width), bf16),
            ),
            in_specs=[pl.BlockSpec(memory_space=pl.ANY)] * 11,
            out_specs=(
                pl.BlockSpec(memory_space=pl.ANY), pl.BlockSpec(memory_space=pltpu.VMEM)
            ),
            scratch_shapes=[
                pltpu.VMEM((2, width, rows_total), bf16),
                pltpu.VMEM((n, 1, rows_total), f32),
                pltpu.VMEM((n, 1, rows_total), f32),
                pltpu.VMEM((devices, VALS, LANES), f32),
                pltpu.VMEM((devices, VALS, LANES), f32),
                pltpu.VMEM((n, width, width), bf16),
                pltpu.VMEM((n, width, width), bf16),
                pltpu.VMEM((n, width, width), bf16),
                pltpu.VMEM((n, width, width), bf16),
                pltpu.VMEM((VALS, total), f32),
                pltpu.VMEM((SG, total), bf16),
                pltpu.VMEM((SG, total), bf16),
                pltpu.VMEM((SG, total), bf16),
                pltpu.VMEM((SG, quarter * width), bf16),
                pltpu.VMEM((SG, SG), bf16),
                pltpu.SemaphoreType.DMA((devices,)),
                pltpu.SemaphoreType.DMA((devices,)),
                pltpu.SemaphoreType.DMA((n,)),
                pltpu.SemaphoreType.DMA((n,)),
                pltpu.SemaphoreType.DMA((n,)),
                pltpu.SemaphoreType.DMA((n,)),
                pltpu.SemaphoreType.DMA((n,)),
                pltpu.VMEM((rows_total, width), bf16),
                pltpu.VMEM((1, n), jnp.int32),
                pltpu.VMEM((1, nvis), jnp.int32),
                pltpu.VMEM((1, nvis), jnp.int32),
                pltpu.VMEM((1, nvis), f32),
                pltpu.VMEM((1, nvis), f32),
                pltpu.VMEM((width, rows_total), f32),
                pltpu.VMEM((width, rows_total), f32),
                pltpu.VMEM((1, rows_total), f32),
                pltpu.VMEM((SG, SG), bf16),
                pltpu.VMEM((quarter * width, SG), bf16),
                pltpu.SemaphoreType.DMA((11,)),
            ],
            compiler_params=pltpu.CompilerParams(
                collective_id=0, has_side_effects=True, vmem_limit_bytes=58 * 1024 * 1024
            ),
        )(
            strips, offsets, vis_subgrid.reshape(1, nvis),
            vis_uv.reshape(1, nvis), observed.reshape(1, nvis), weights.reshape(1, nvis),
            jnp.asarray(cas), jnp.asarray(dif), jnp.asarray(taper),
            jnp.asarray(ctab), jnp.asarray(cplace),
        )
        chunk = min(2048, rows_total)
        return pl.pallas_call(
            finish,
            out_shape=jax.ShapeDtypeStruct((rows_total, width), f32),
            grid=(rows_total // chunk,),
            in_specs=[
                pl.BlockSpec((width, n * width), lambda i: (0, 0)),
                pl.BlockSpec((n * width, chunk), lambda i: (0, i)),
            ],
            out_specs=pl.BlockSpec((chunk, width), lambda i: (i, 0)),
            compiler_params=pltpu.CompilerParams(vmem_limit_bytes=58 * 1024 * 1024),
        )(returned, tables)

    in_specs = (
        P("facet", "col"),
        P("col", None),
        P(("facet", "col")),
        P(("facet", "col")),
        P(("facet", "col")),
        P(("facet", "col")),
    )
    return jax.shard_map(
        per_device, mesh=mesh, in_specs=in_specs, out_specs=P("facet", "col"), check_vma=False
    )
```
